32 devices in a mesh: seq: 8 (over y, x, core), head: 2 (over z_hi), var: 2 (over z_lo).
Axes of the slice: x: 2, y: 2, z: 4 (z_hi: 2, z_lo: 2; z = z_hi * 2 + z_lo), core: 2. Of those that a mesh axis runs over, the one named last changes fastest.
Arguments:
- inner: bfloat16 [512, 1024], P('seq', 'head'), may hold values from -4.5 to 4.5
- residual_in: bfloat16 [512, 4096], P('seq', 'head'), may hold values from -6 to 6
- erase: int32 [2, 512], P('var', 'seq'), parts along dimension 0, may hold values from 0 to 1, as said below
- conv_weight: float32 [4, 1024], P(None, 'head'), may hold values from -3 to 3
- qkv_weight: bfloat16 [2, 512, 1536], P('head'), may hold values from -0.25 to 0.25
- gate_weight: bfloat16 [2, 2, 512], P('head'), may hold values from -0.4075734 to 0.4075734, as said below
- gate_bias: float32 [2, 2], P('head'), as said below
- norm_gain: float32 [1024], P('head'), may hold values from 0.5 to 1.5
- down_weight: bfloat16 [1024, 4096], P('head', 'seq'), may hold values from -0.1875 to 0.1875
Outputs:
- mixed: bfloat16 [2, 512, 4096], P('var', 'seq', 'head'), parts along dimension 0
The draws below stay inside these ranges and needn't reach their ends.
There are 2 independent parts, one for each index of `var`. The reference program is written for one: setup_inputs(seed, part) draws one part's arguments, and reference() takes and returns one part's arrays. A program takes and returns all parts, laid end to end along the dimension named above; an argument that names none is the same for every part. Nothing has to cross between parts.
Inputs may be any that keep to these rules, and one draw needn't show every extreme that they name: `erase`: each variant erases a few runs of consecutive tokens. `gate_weight`: row 0 of each head holds the input gate projection and row 1 the forget gate projection. `gate_bias`: column 0 is the input gate bias and column 1 the forget gate bias of each head.
All inputs are finite; a program needn't handle non-finite values.
Results may differ from the reference program's by a relative error of at most 0.014.
Values may be sent and summed in bfloat16 or wider, within the bound.
A program may use at most 128 MiB of HBM per device.

```python
import jax
import jax.numpy as jnp
from jax import lax

D = 4096
DH = 512
CONV = 4
VARS = 1
TOK_DEV = 64
HEADS = 2
INNER = 1024
TOKENS = 512
N_SEQ = 8


def draw_inner(key, part):
    base_key = jax.random.fold_in(key, 31)
    entries = jnp.clip(jax.random.normal(base_key, (TOKENS, INNER)), -4.5, 4.5)
    return entries.astype(jnp.float32).astype(jnp.bfloat16)


def draw_gate_weight(key, part):
    base_key = jax.random.fold_in(key, 37)
    spread = max(DH // 9, 1) ** (-0.5)
    entries = jnp.clip(jax.random.normal(base_key, (HEADS, 2, DH)), -3.0, 3.0)
    row_scale = jnp.array([0.02, 1.0], jnp.float32)[None, :, None]
    return (entries.astype(jnp.float32) * spread * row_scale).astype(jnp.bfloat16)


def draw_erase(key, part):
    first_key, second_key = jax.random.split(jax.random.fold_in(key, 11), 2)
    span_starts = jax.random.randint(first_key, (VARS, 6), 0, TOKENS)
    span_lengths = jax.random.randint(second_key, (VARS, 6), 1, max(2, TOKENS // 16))
    position = jnp.arange(TOKENS)[None, :, None]
    covered = (position >= span_starts[:, None, :]) & (position < span_starts[:, None, :] + span_lengths[:, None, :])
    return jnp.any(covered, axis=2).astype(jnp.int32)


def draw_gate_bias(key, part):
    order_key, slow_key, fast_key, input_key = jax.random.split(jax.random.fold_in(key, 23), 4)
    order = jax.random.permutation(order_key, HEADS)
    slow_heads = order < max(HEADS // 2, 1)
    slow_bias = jnp.log(TOKENS * 1.0) + jax.random.uniform(slow_key, (HEADS,), minval=0.3, maxval=0.8)
    fast_bias = jax.random.uniform(fast_key, (HEADS,), minval=3.2, maxval=4.2)
    forget_bias = jnp.where(slow_heads, slow_bias, fast_bias)
    input_bias = jax.random.uniform(input_key, (HEADS,), minval=-1.0, maxval=1.0)
    return jnp.stack([input_bias, forget_bias], axis=1).astype(jnp.float32)


def steps_of(own_key, extent, shards, smallest, top_value):
    gain, own = 1.0, jax.random.fold_in(own_key, 6)
    for dim, parts in shards:
        draws = jnp.exp(jax.random.uniform(jax.random.fold_in(own, dim), (parts,), jnp.float32, smallest / len(shards), top_value / len(shards)))
        gain = gain * jnp.repeat(draws, extent[dim] // parts).reshape([-1 if axis == dim else 1 for axis in range(len(extent))])
    return gain


def gaussian(key, dims, scale, bound, pieces=(), kind=jnp.bfloat16):
    loudness = steps_of(key, dims, pieces, -0.22, 0.18) if pieces else 1.0
    values = jax.random.normal(key, dims, jnp.float32) * scale * loudness
    return jnp.minimum(jnp.maximum(values, -bound), bound).astype(kind)


def setup_inputs(seed: int = 0, part: int = 0) -> dict:
    keys = jax.random.split(jax.random.key(seed), 10)
    part_keys = jax.random.split(jax.random.fold_in(keys[9], part), 10)
    inner = draw_inner(jax.random.fold_in(keys[9], 71), part)
    residual_in = gaussian(keys[1], (TOKENS, D), 1.0, 6.0, ((0, 8), (1, 2)))
    erase = draw_erase(jax.random.fold_in(jax.random.fold_in(keys[9], part), 71), part)
    conv_weight = gaussian(keys[3], (CONV, INNER), 0.5, 3.0, ((1, 2),), jnp.float32)
    qkv_weight = gaussian(keys[4], (HEADS, DH, 3 * DH), DH ** -0.5, 0.25, ((0, 2),))
    gate_weight = draw_gate_weight(jax.random.fold_in(keys[9], 71), part)
    gate_bias = draw_gate_bias(jax.random.fold_in(keys[9], 71), part)
    norm_gain = jnp.clip(1.0 + 0.1 * jax.random.normal(keys[7], (INNER,), jnp.float32), 0.5, 1.5)
    down_weight = gaussian(keys[8], (INNER, D), INNER ** -0.5, 0.1875, ((0, 2), (1, 8)))
    return dict(inner=inner, residual_in=residual_in, erase=erase, conv_weight=conv_weight, qkv_weight=qkv_weight, gate_weight=gate_weight, gate_bias=gate_bias, norm_gain=norm_gain, down_weight=down_weight)


def reference(inner, residual_in, erase, conv_weight, qkv_weight, gate_weight, gate_bias, norm_gain, down_weight):
    kept_mask = (1 - erase).astype(jnp.bfloat16)
    erased = inner[None, :, :] * kept_mask[:, :, None]
    padded = jnp.pad(erased, ((0, 0), (CONV - 1, 0), (0, 0)))
    conv_taps = conv_weight.astype(jnp.float32)
    proj_all = qkv_weight.astype(jnp.float32)
    gate_all = gate_weight.astype(jnp.float32)
    gain_heads = norm_gain.astype(jnp.float32).reshape(HEADS, DH)
    causal = jnp.arange(TOK_DEV)[:, None] >= jnp.arange(TOK_DEV)[None, :]

    def block(memory, block_index):
        row_start = (block_index * TOK_DEV).astype(jnp.int32)
        window = lax.dynamic_slice_in_dim(padded, row_start, TOK_DEV + CONV - 1, 1).astype(jnp.float32)
        convolved = jnp.zeros((VARS, TOK_DEV, INNER), jnp.float32)
        for offset in range(CONV):
            convolved = convolved + conv_taps[offset] * window[:, CONV - 1 - offset:CONV - 1 - offset + TOK_DEV]
        activated = jax.nn.silu(convolved).astype(jnp.bfloat16).astype(jnp.float32).reshape(VARS, TOK_DEV, HEADS, DH)
        own_rows = window[:, CONV - 1:].reshape(VARS, TOK_DEV, HEADS, DH)
        query_key = jnp.einsum('vthd,hde->vthe', activated, proj_all[:, :, :2 * DH])
        queries = query_key[..., :DH].astype(jnp.bfloat16).astype(jnp.float32)
        key_rows = (query_key[..., DH:] * DH ** (-0.5)).astype(jnp.bfloat16).astype(jnp.float32)
        values = jnp.einsum('vthd,hde->vthe', own_rows, proj_all[:, :, 2 * DH:]).astype(jnp.bfloat16).astype(jnp.float32)
        gate_pre = jnp.einsum('vthd,hgd->vthg', activated, gate_all) + gate_bias.astype(jnp.float32)
        input_log = 15.0 * jnp.tanh(gate_pre[..., 0] / 15.0)
        forget_log = jax.nn.log_sigmoid(gate_pre[..., 1])
        cumulated = jnp.cumsum(forget_log, axis=1)
        block_decay = cumulated[:, -1]
        scores = jnp.einsum('vthd,vshd->vhts', queries, key_rows)
        cum_heads = jnp.transpose(cumulated, (0, 2, 1))
        in_heads = jnp.transpose(input_log, (0, 2, 1))
        exponent = cum_heads[:, :, :, None] - cum_heads[:, :, None, :] + in_heads[:, :, None, :]
        weights = (scores * jnp.exp(jnp.where(causal, exponent, -jnp.inf))).astype(jnp.bfloat16).astype(jnp.float32)
        intra_part = jnp.einsum('vhts,vshe->vthe', weights, values)
        memory_rounded = lax.optimization_barrier(memory.astype(jnp.bfloat16)).astype(jnp.float32)
        carry_part = jnp.einsum('vthd,vhde->vthe', queries, memory_rounded)
        numerator = jnp.exp(cumulated)[..., None] * carry_part + intra_part
        key_scale = jnp.exp(block_decay[:, None, :] - cumulated + input_log)
        scaled_keys = (key_scale[..., None] * key_rows).astype(jnp.bfloat16).astype(jnp.float32)
        own_memory = jnp.einsum('vshd,vshe->vhde', scaled_keys, values)
        memory = jnp.exp(block_decay)[:, :, None, None] * memory + own_memory
        row_mean = lax.optimization_barrier(jnp.mean(numerator, axis=-1, keepdims=True))
        centred = numerator - row_mean
        row_var = lax.optimization_barrier(jnp.mean(centred * centred, axis=-1, keepdims=True))
        normed = (centred * lax.rsqrt(row_var + 1e-05) * gain_heads).astype(jnp.bfloat16)
        return (memory, normed.reshape(VARS, TOK_DEV, INNER))
    start_memory = jnp.zeros((VARS, HEADS, DH, DH), jnp.float32)
    final_memory, blocks = lax.scan(block, start_memory, jnp.arange(N_SEQ, dtype=jnp.int32))
    normed_all = jnp.transpose(blocks, (1, 0, 2, 3)).reshape(VARS * TOKENS, INNER)

    def add_head(head_index, running_sum):
        head_start = (head_index * DH).astype(jnp.int32)
        head_rows = lax.dynamic_slice_in_dim(normed_all, head_start, DH, 1)
        head_weight = lax.dynamic_slice_in_dim(down_weight, head_start, DH, 0)
        head_part = jnp.dot(head_rows, head_weight, preferred_element_type=jnp.float32).astype(jnp.bfloat16)
        head_part = lax.optimization_barrier(head_part)
        return running_sum + head_part.astype(jnp.float32)
    running_sum = lax.fori_loop(0, HEADS, add_head, jnp.zeros((VARS * TOKENS, D), jnp.float32))
    mixed = residual_in[None, :, :].astype(jnp.float32) + running_sum.reshape(VARS, TOKENS, D)
    return mixed.astype(jnp.bfloat16)
```

```python
import functools

import jax
import jax.numpy as jnp
from jax import lax
from jax.experimental import pallas as pl
from jax.experimental.pallas import tpu as pltpu
from jax.sharding import PartitionSpec as P

CONV = 4
PAD = 16
GROUP = 4
MESH = pl.DeviceIdType.MESH
BF16 = jnp.bfloat16
F32 = jnp.float32


def dot_nt(a, b):
    return lax.dot_general(a, b, (((1,), (1,)), ((), ())), preferred_element_type=F32)


def dot_nn(a, b):
    return jnp.dot(a, b, preferred_element_type=F32)


def as_column(row, eye):
    return jnp.sum(jnp.where(eye, row, 0.0), axis=1, keepdims=True)


def kernel(
    n_seq,
    n_head,
    inner_ref,
    erase_ref,
    conv_ref,
    gate_ref,
    bias_ref,
    gain_ref,
    proj_hbm,
    down_hbm,
    resid_hbm,
    out_ref,
    rows,
    proj,
    down,
    resid,
    keys,
    vals,
    tails,
    part,
    landed,
    load_sem,
    row_send,
    row_recv,
    part_send,
    part_recv,
    self_sem,
):
    seq, head = lax.axis_index("seq"), lax.axis_index("head")
    tok, width = inner_ref.shape
    columns = down.shape[1]
    per_head = n_seq // n_head
    chunk = GROUP * tok
    chunks = n_seq // GROUP
    small = chunks <= 2
    out_head, out_slot = seq // per_head, lax.rem(seq, per_head)

    def loop(count, step, carry=None):
        if small:
            for position in range(count):
                carry = step(position, carry)
            return carry
        return lax.fori_loop(0, count, step, carry)

    barrier = pltpu.get_barrier_semaphore()
    group = n_seq * n_head
    flat = seq * n_head + head

    def greet(step, carry):
        other = lax.rem(flat + step + 1, group)
        pl.semaphore_signal(
            barrier,
            inc=1,
            device_id={"seq": other // n_head, "head": lax.rem(other, n_head)},
            device_id_type=MESH,
        )
        return carry

    loop(group - 1, greet, 0)

    loads = [
        pltpu.make_async_copy(proj_hbm.at[0], proj, load_sem.at[0]),
        pltpu.make_async_copy(down_hbm, down, load_sem.at[1]),
        pltpu.make_async_copy(resid_hbm, resid, load_sem.at[2]),
    ]
    for load in loads:
        load.start()

    rows[pl.ds(0, PAD), :] = jnp.zeros((PAD, width), BF16)
    line = lax.broadcasted_iota(jnp.int32, (tok, tok), 0)
    lane = lax.broadcasted_iota(jnp.int32, (tok, tok), 1)
    kept = as_column((1 - erase_ref[...]).astype(F32), line == lane)
    own = pl.ds(pl.multiple_of(PAD + seq * tok, PAD), tok)
    rows[own, :] = (inner_ref[...].astype(F32) * kept).astype(BF16)

    pl.semaphore_wait(barrier, group - 1)

    def row_copy(block, target):
        place = pl.ds(pl.multiple_of(PAD + block * tok, PAD), tok)
        return pltpu.make_async_remote_copy(
            src_ref=rows.at[place],
            dst_ref=rows.at[place],
            send_sem=row_send.at[target],
            recv_sem=row_recv.at[block],
            device_id={"seq": target},
            device_id_type=MESH,
        )

    def send_rows(step, carry):
        row_copy(seq, lax.rem(seq + step + 1, n_seq)).start()
        return carry

    loop(n_seq - 1, send_rows, 0)

    line = lax.broadcasted_iota(jnp.int32, (chunk, chunk), 0)
    lane = lax.broadcasted_iota(jnp.int32, (chunk, chunk), 1)
    loads[0].wait()
    loads[1].wait()

    def part_copy(block, slot):
        return pltpu.make_async_remote_copy(
            src_ref=part.at[block],
            dst_ref=landed.at[head, out_slot],
            send_sem=part_send.at[block],
            recv_sem=part_recv.at[head, out_slot],
            device_id={"seq": block, "head": out_head},
            device_id_type=MESH,
        )

    def work(index, carry):
        start = index * chunk if small else pl.multiple_of(index * chunk, chunk)
        here = pl.ds(start, chunk)
        for position in range(GROUP):
            block = index * GROUP + position

            @pl.when(block != seq)
            def _():
                row_copy(block, lax.rem(seq + 1, n_seq)).wait_recv()

        window = rows[pl.ds(start, chunk + PAD), :].astype(F32)
        convolved = conv_ref[pl.ds(0, 1), :] * window[PAD:]
        for offset in range(1, CONV):
            convolved += conv_ref[pl.ds(offset, 1), :] * pltpu.roll(window, offset, 0)[PAD:]
        half = 0.5 * convolved
        activated = (half + half * jnp.tanh(half)).astype(BF16)
        erased = rows[pl.ds(start + PAD, chunk), :]
        gates = dot_nt(gate_ref[0], activated)
        input_log = 15.0 * jnp.tanh((gates[0:1] + bias_ref[0, 0]) / 15.0)
        forget = gates[1:2] + bias_ref[0, 1]
        forget_log = jnp.minimum(forget, 0.0) - jnp.log1p(jnp.exp(-jnp.abs(forget)))
        summed = jnp.dot(
            jnp.broadcast_to(forget_log, (8, chunk)),
            (line <= lane).astype(F32),
            preferred_element_type=F32,
            precision=lax.Precision.HIGHEST,
        )
        cumulated = summed[0:1]
        last = summed[0:1, chunk - 1 : chunk]
        by_row = as_column(cumulated, line == lane)
        queries = dot_nn(activated, proj[:, :width]).astype(BF16)
        key_rows = (dot_nn(activated, proj[:, width : 2 * width]) * width ** (-0.5)).astype(BF16)
        values = dot_nn(erased, proj[:, 2 * width :]).astype(BF16)
        keys[here, :] = key_rows
        vals[here, :] = values
        exponent = by_row + (input_log - cumulated)
        weights = dot_nt(queries, key_rows) * jnp.exp(jnp.where(line >= lane, exponent, -jnp.inf))
        numerator = dot_nn(weights.astype(BF16), values)

        def earlier(other, total):
            there = pl.ds(other * chunk if small else pl.multiple_of(other * chunk, chunk), chunk)
            tail = tails[other]
            scores = dot_nt(queries, keys[there, :])
            weights = (scores * jnp.exp(by_row + tail[0:1])).astype(BF16)
            tails[other] = tail + last
            return total + dot_nn(weights, vals[there, :])

        numerator = loop(index, earlier, numerator)
        tails[index] = jnp.broadcast_to(last - cumulated + input_log, (8, chunk))
        mean = jnp.mean(numerator, axis=1, keepdims=True)
        centred = numerator - mean
        variance = jnp.mean(centred * centred, axis=1, keepdims=True)
        normed = (centred * lax.rsqrt(variance + 1e-05) * gain_ref[...]).astype(BF16)
        product = dot_nn(normed, down[...]).astype(BF16)
        for position in range(GROUP):
            block = index * GROUP + position
            part[block] = product[position * tok : (position + 1) * tok]
            mine = (block == seq) & (out_head == head)

            @pl.when(jnp.logical_not(mine))
            def _():
                part_copy(block, 0).start()

            @pl.when(mine)
            def _():
                pltpu.make_async_copy(part.at[block], landed.at[head, out_slot], self_sem).start()

        return carry

    loop(chunks, work, 0)
    loads[2].wait()

    for slot in range(per_head):
        for other in range(n_head):
            source = head * per_head + slot
            mine = (source == seq) & (other == head)

            @pl.when(jnp.logical_not(mine))
            def _():
                pltpu.make_async_remote_copy(
                    src_ref=part.at[0],
                    dst_ref=landed.at[other, slot],
                    send_sem=part_send.at[0],
                    recv_sem=part_recv.at[other, slot],
                    device_id={"seq": lax.rem(seq + 1, n_seq)},
                    device_id_type=MESH,
                ).wait_recv()

            @pl.when(mine)
            def _():
                pltpu.make_async_copy(part.at[0], landed.at[head, out_slot], self_sem).wait()

        total = landed[0, slot].astype(F32)
        for other in range(1, n_head):
            total += landed[other, slot].astype(F32)
        place = pl.ds(slot * columns, columns)
        out_ref[0, :, place] = (resid[:, place].astype(F32) + total).astype(BF16)

    def sent_rows(step, carry):
        row_copy(seq, lax.rem(seq + step + 1, n_seq)).wait_send()
        return carry

    loop(n_seq - 1, sent_rows, 0)

    def sent_parts(block, carry):
        @pl.when(jnp.logical_not((block == seq) & (out_head == head)))
        def _():
            part_copy(block, 0).wait_send()

        return carry

    loop(n_seq, sent_parts, 0)


def body(
    n_seq,
    n_head,
    inner,
    residual_in,
    erase,
    conv_weight,
    qkv_weight,
    gate_weight,
    gate_bias,
    norm_gain,
    down_weight,
):
    tok, width = inner.shape
    columns = down_weight.shape[1]
    tokens = tok * n_seq
    chunk = GROUP * tok
    vmem = pl.BlockSpec(memory_space=pltpu.VMEM)
    anywhere = pl.BlockSpec(memory_space=pl.ANY)
    return pl.pallas_call(
        functools.partial(kernel, n_seq, n_head),
        out_shape=jax.ShapeDtypeStruct((1, tok, residual_in.shape[1]), BF16),
        in_specs=[vmem] * 4 + [pl.BlockSpec(memory_space=pltpu.SMEM), vmem] + [anywhere] * 3,
        out_specs=vmem,
        scratch_shapes=[
            pltpu.VMEM((PAD + tokens, width), BF16),
            pltpu.VMEM(qkv_weight.shape[1:], BF16),
            pltpu.VMEM(down_weight.shape, BF16),
            pltpu.VMEM(residual_in.shape, BF16),
            pltpu.VMEM((tokens, width), BF16),
            pltpu.VMEM((tokens, width), BF16),
            pltpu.VMEM((tokens // chunk, 8, chunk), F32),
            pltpu.VMEM((n_seq, tok, columns), BF16),
            pltpu.VMEM((n_head, n_seq // n_head, tok, columns), BF16),
            pltpu.SemaphoreType.DMA((3,)),
            pltpu.SemaphoreType.DMA((n_seq,)),
            pltpu.SemaphoreType.DMA((n_seq,)),
            pltpu.SemaphoreType.DMA((n_seq,)),
            pltpu.SemaphoreType.DMA((n_head, n_seq // n_head)),
            pltpu.SemaphoreType.DMA,
        ],
        compiler_params=pltpu.CompilerParams(
            collective_id=0, has_side_effects=True, vmem_limit_bytes=48 * 2**20
        ),
    )(
        inner,
        erase,
        conv_weight,
        gate_weight,
        gate_bias,
        norm_gain.reshape(1, width),
        qkv_weight,
        down_weight,
        residual_in,
    )


def solution(mesh):
    in_specs = (
        P("seq", "head"),
        P("seq", "head"),
        P("var", "seq"),
        P(None, "head"),
        P("head", None, None),
        P("head", None, None),
        P("head", None),
        P("head"),
        P("head", "seq"),
    )
    out_specs = P("var", "seq", "head")
    run = functools.partial(body, mesh.shape["seq"], mesh.shape["head"])
    return jax.shard_map(run, mesh=mesh, in_specs=in_specs, out_specs=out_specs, check_vma=False)
```

```python
import functools

import jax
import jax.numpy as jnp
from jax import lax
from jax.experimental import pallas as pl
from jax.experimental.pallas import tpu as pltpu
from jax.sharding import PartitionSpec as P

CONV = 4
PAD = 16
GROUP = 4
MESH = pl.DeviceIdType.MESH
BF16 = jnp.bfloat16
F32 = jnp.float32


def dot_nt(a, b):
    return lax.dot_general(a, b, (((1,), (1,)), ((), ())), preferred_element_type=F32)


def dot_nn(a, b):
    return jnp.dot(a, b, preferred_element_type=F32)


def as_column(row, eye):
    return jnp.sum(jnp.where(eye, row, 0.0), axis=1, keepdims=True)


def kernel(
    n_seq,
    n_head,
    inner_hbm,
    erase_hbm,
    conv_hbm,
    gate_hbm,
    bias_ref,
    gain_hbm,
    proj_hbm,
    down_hbm,
    resid_hbm,
    out_ref,
    inner,
    erase,
    conv,
    gate,
    gain,
    proj,
    down,
    given,
    resid,
    rows,
    keys,
    vals,
    tails,
    part,
    landed,
    load_sem,
    row_send,
    row_recv,
    down_sem,
    part_send,
    part_recv,
    self_sem,
):
    seq, head = lax.axis_index("seq"), lax.axis_index("head")
    tok, width = inner.shape
    sides, _, piece = down.shape
    per_head = n_seq // n_head
    chunk = GROUP * tok
    chunks = n_seq // GROUP
    small = chunks <= 2
    out_head, out_slot = seq // per_head, lax.rem(seq, per_head)
    swap = sides == 2
    partner = lax.rem(seq + n_seq // 2, n_seq)
    sibling = seq + 1 - 2 * lax.rem(seq, 2)

    def loop(count, step, carry=None):
        if small:
            for position in range(count):
                carry = step(position, carry)
            return carry
        return lax.fori_loop(0, count, step, carry)

    loads = [
        pltpu.make_async_copy(source, target, load_sem.at[index])
        for index, (source, target) in enumerate(
            [
                (inner_hbm, inner),
                (erase_hbm, erase),
                (down_hbm.at[:, pl.ds((sides - 1) * piece, piece)], given if swap else down.at[0]),
                (proj_hbm.at[0], proj),
                (conv_hbm, conv),
                (gate_hbm.at[0], gate),
                (gain_hbm, gain),
                (resid_hbm, resid),
            ]
            + ([(down_hbm.at[:, pl.ds(0, piece)], down.at[0])] if swap else [])
        )
    ]
    for load in loads:
        load.start()

    barrier = pltpu.get_barrier_semaphore()
    group = n_seq * n_head
    flat = seq * n_head + head

    def greet(step, carry):
        other = lax.rem(flat + step + 1, group)
        pl.semaphore_signal(
            barrier,
            inc=1,
            device_id={"seq": other // n_head, "head": lax.rem(other, n_head)},
            device_id_type=MESH,
        )
        return carry

    loop(group - 1, greet, 0)

    rows[pl.ds(0, PAD), :] = jnp.zeros((PAD, width), BF16)
    line = lax.broadcasted_iota(jnp.int32, (tok, tok), 0)
    lane = lax.broadcasted_iota(jnp.int32, (tok, tok), 1)
    loads[0].wait()
    loads[1].wait()
    kept = as_column((1 - erase[...]).astype(F32), line == lane)
    own = pl.ds(pl.multiple_of(PAD + seq * tok, PAD), tok)
    rows[own, :] = (inner[...].astype(F32) * kept).astype(BF16)
    for load in loads[2:]:
        load.wait()

    pl.semaphore_wait(barrier, group - 1)

    def row_copy(block, target, slot):
        place = pl.ds(pl.multiple_of(PAD + block * tok, PAD), tok)
        return pltpu.make_async_remote_copy(
            src_ref=rows.at[place],
            dst_ref=rows.at[place],
            send_sem=row_send.at[slot],
            recv_sem=row_recv.at[block],
            device_id={"seq": target},
            device_id_type=MESH,
        )

    def send_rows(step, carry):
        row_copy(seq, lax.rem(seq + 2 * step + 2, n_seq), step).start()
        return carry

    loop(n_seq // 2 - 1, send_rows, 0)
    row_copy(seq, sibling, n_seq // 2 - 1).start()
    give = pltpu.make_async_remote_copy(
        src_ref=given if swap else down.at[0],
        dst_ref=down.at[sides - 1],
        send_sem=down_sem.at[0],
        recv_sem=down_sem.at[1],
        device_id={"seq": partner},
        device_id_type=MESH,
    )
    if swap:
        give.start()

    def forward(step, carry):
        block = lax.rem(seq + n_seq - 2 * step - 2, n_seq)
        row_copy(block, sibling, 0).wait_recv()
        row_copy(block, sibling, n_seq // 2 + step).start()
        return carry

    loop(n_seq // 2 - 1, forward, 0)

    line = lax.broadcasted_iota(jnp.int32, (chunk, chunk), 0)
    lane = lax.broadcasted_iota(jnp.int32, (chunk, chunk), 1)

    def part_copy(side, block, target):
        return pltpu.make_async_remote_copy(
            src_ref=part.at[side, block],
            dst_ref=landed.at[head, side, out_slot],
            send_sem=part_send.at[side, block],
            recv_sem=part_recv.at[head, side, out_slot],
            device_id={"seq": block, "head": target},
            device_id_type=MESH,
        )

    if swap:
        first = 1 - lax.rem(out_head + head, 2)
        routes = [(first, 1 - head), (1 - first, head)]
    else:
        routes = [(0, out_head)]

    def work(index, carry):
        start = index * chunk if small else pl.multiple_of(index * chunk, chunk)
        here = pl.ds(start, chunk)
        for position in range(GROUP):
            block = index * GROUP + position

            @pl.when(lax.rem(seq + block, 2) == 1)
            def _():
                row_copy(block, sibling, 0).wait_recv()

        window = rows[pl.ds(start, chunk + PAD), :].astype(F32)
        convolved = conv[pl.ds(0, 1), :] * window[PAD:]
        for offset in range(1, CONV):
            convolved += conv[pl.ds(offset, 1), :] * pltpu.roll(window, offset, 0)[PAD:]
        half = 0.5 * convolved
        activated = (half + half * jnp.tanh(half)).astype(BF16)
        erased = rows[pl.ds(start + PAD, chunk), :]
        gates = dot_nt(gate[...], activated)
        input_log = 15.0 * jnp.tanh((gates[0:1] + bias_ref[0, 0]) / 15.0)
        forget = gates[1:2] + bias_ref[0, 1]
        forget_log = jnp.minimum(forget, 0.0) - jnp.log1p(jnp.exp(-jnp.abs(forget)))
        summed = jnp.dot(
            jnp.broadcast_to(forget_log, (8, chunk)),
            (line <= lane).astype(F32),
            preferred_element_type=F32,
            precision=lax.Precision.HIGHEST,
        )
        cumulated = summed[0:1]
        last = summed[0:1, chunk - 1 : chunk]
        by_row = as_column(cumulated, line == lane)
        queries = dot_nn(activated, proj[:, :width]).astype(BF16)
        key_rows = (dot_nn(activated, proj[:, width : 2 * width]) * width ** (-0.5)).astype(BF16)
        values = dot_nn(erased, proj[:, 2 * width :]).astype(BF16)
        keys[here, :] = key_rows
        vals[here, :] = values
        exponent = by_row + (input_log - cumulated)
        weights = dot_nt(queries, key_rows) * jnp.exp(jnp.where(line >= lane, exponent, -jnp.inf))
        numerator = dot_nn(weights.astype(BF16), values)

        def earlier(other, total):
            there = pl.ds(other * chunk if small else pl.multiple_of(other * chunk, chunk), chunk)
            tail = tails[other]
            scores = dot_nt(queries, keys[there, :])
            weights = (scores * jnp.exp(by_row + tail[0:1])).astype(BF16)
            tails[other] = tail + last
            return total + dot_nn(weights, vals[there, :])

        numerator = loop(index, earlier, numerator)
        tails[index] = jnp.broadcast_to(last - cumulated + input_log, (8, chunk))
        mean = jnp.mean(numerator, axis=1, keepdims=True)
        centred = numerator - mean
        variance = jnp.mean(centred * centred, axis=1, keepdims=True)
        normed = (centred * lax.rsqrt(variance + 1e-05) * gain[...]).astype(BF16)
        if swap:

            @pl.when(index == 0)
            def _():
                give.wait_recv()

        for side, target in routes:
            product = dot_nn(normed, down[side]).astype(BF16)
            for position in range(GROUP):
                block = index * GROUP + position
                part[side, block] = product[position * tok : (position + 1) * tok]
                mine = (block == seq) & (target == head)

                @pl.when(jnp.logical_not(mine))
                def _():
                    part_copy(side, block, target).start()

                @pl.when(mine)
                def _():
                    pltpu.make_async_copy(
                        part.at[side, block], landed.at[head, side, out_slot], self_sem
                    ).start()

        return carry

    loop(chunks, work, 0)

    for slot in range(per_head):
        for side in range(sides):
            source = lax.rem(head + side, n_head) * per_head + slot
            for other in range(n_head):
                mine = (source == seq) & (other == head)

                @pl.when(jnp.logical_not(mine))
                def _():
                    pltpu.make_async_remote_copy(
                        src_ref=part.at[0, 0],
                        dst_ref=landed.at[other, side, slot],
                        send_sem=part_send.at[0, 0],
                        recv_sem=part_recv.at[other, side, slot],
                        device_id={"seq": sibling},
                        device_id_type=MESH,
                    ).wait_recv()

                @pl.when(mine)
                def _():
                    pltpu.make_async_copy(part.at[0, 0], landed.at[0, 0, 0], self_sem).wait()

            total = landed[0, side, slot].astype(F32)
            for other in range(1, n_head):
                total += landed[other, side, slot].astype(F32)
            place = pl.ds((slot * sides + side) * piece, piece)
            out_ref[0, :, place] = (resid[:, place].astype(F32) + total).astype(BF16)

    def sent_rows(step, carry):
        row_copy(seq, sibling, step).wait_send()
        return carry

    loop(n_seq - 1, sent_rows, 0)
    if swap:
        give.wait_send()

    def sent_parts(block, carry):
        for side, target in routes:

            @pl.when(jnp.logical_not((block == seq) & (target == head)))
            def _():
                part_copy(side, block, target).wait_send()

        return carry

    loop(n_seq, sent_parts, 0)


def body(
    n_seq,
    n_head,
    inner,
    residual_in,
    erase,
    conv_weight,
    qkv_weight,
    gate_weight,
    gate_bias,
    norm_gain,
    down_weight,
):
    tok, width = inner.shape
    columns = down_weight.shape[1]
    tokens = tok * n_seq
    chunk = GROUP * tok
    sides = 2 if n_head == 2 and columns % 256 == 0 else 1
    piece = columns // sides
    per_head = n_seq // n_head
    vmem = pl.BlockSpec(memory_space=pltpu.VMEM)
    anywhere = pl.BlockSpec(memory_space=pl.ANY)
    return pl.pallas_call(
        functools.partial(kernel, n_seq, n_head),
        out_shape=jax.ShapeDtypeStruct((1, tok, residual_in.shape[1]), BF16),
        in_specs=[anywhere] * 4 + [pl.BlockSpec(memory_space=pltpu.SMEM)] + [anywhere] * 4,
        out_specs=vmem,
        scratch_shapes=[
            pltpu.VMEM(inner.shape, BF16),
            pltpu.VMEM(erase.shape, jnp.int32),
            pltpu.VMEM(conv_weight.shape, F32),
            pltpu.VMEM(gate_weight.shape[1:], BF16),
            pltpu.VMEM((1, width), F32),
            pltpu.VMEM(qkv_weight.shape[1:], BF16),
            pltpu.VMEM((sides, width, piece), BF16),
            pltpu.VMEM((width, piece), BF16),
            pltpu.VMEM(residual_in.shape, BF16),
            pltpu.VMEM((PAD + tokens, width), BF16),
            pltpu.VMEM((tokens, width), BF16),
            pltpu.VMEM((tokens, width), BF16),
            pltpu.VMEM((tokens // chunk, 8, chunk), F32),
            pltpu.VMEM((sides, n_seq, tok, piece), BF16),
            pltpu.VMEM((n_head, sides, per_head, tok, piece), BF16),
            pltpu.SemaphoreType.DMA((9,)),
            pltpu.SemaphoreType.DMA((n_seq,)),
            pltpu.SemaphoreType.DMA((n_seq,)),
            pltpu.SemaphoreType.DMA((2,)),
            pltpu.SemaphoreType.DMA((sides, n_seq)),
            pltpu.SemaphoreType.DMA((n_head, sides, per_head)),
            pltpu.SemaphoreType.DMA,
        ],
        compiler_params=pltpu.CompilerParams(
            collective_id=0, has_side_effects=True, vmem_limit_bytes=62 * 2**20
        ),
    )(
        inner,
        erase,
        conv_weight,
        gate_weight,
        gate_bias,
        norm_gain.reshape(1, width),
        qkv_weight,
        down_weight,
        residual_in,
    )


def solution(mesh):
    in_specs = (
        P("seq", "head"),
        P("seq", "head"),
        P("var", "seq"),
        P(None, "head"),
        P("head", None, None),
        P("head", None, None),
        P("head", None),
        P("head"),
        P("head", "seq"),
    )
    out_specs = P("var", "seq", "head")
    run = functools.partial(body, mesh.shape["seq"], mesh.shape["head"])
    return jax.shard_map(run, mesh=mesh, in_specs=in_specs, out_specs=out_specs, check_vma=False)
```

```python
import functools

import jax
import jax.numpy as jnp
from jax import lax
from jax.experimental import pallas as pl
from jax.experimental.pallas import tpu as pltpu
from jax.sharding import PartitionSpec as P

CONV = 4
PAD = 16
GROUP = 4
MESH = pl.DeviceIdType.MESH
BF16 = jnp.bfloat16
F32 = jnp.float32


def dot_nt(a, b):
    return lax.dot_general(a, b, (((1,), (1,)), ((), ())), preferred_element_type=F32)


def dot_nn(a, b):
    return jnp.dot(a, b, preferred_element_type=F32)


def as_column(row, eye):
    return jnp.sum(jnp.where(eye, row, 0.0), axis=1, keepdims=True)


def kernel(
    n_seq,
    n_head,
    inner_hbm,
    erase_hbm,
    conv_hbm,
    gate_hbm,
    bias_ref,
    gain_hbm,
    proj_hbm,
    down_hbm,
    resid_hbm,
    out_ref,
    inner,
    erase,
    conv,
    gate,
    gain,
    proj,
    down,
    given,
    resid,
    rows,
    keys,
    vals,
    tails,
    part,
    landed,
    load_sem,
    row_send,
    row_recv,
    down_sem,
    part_send,
    part_recv,
    self_sem,
):
    seq, head = lax.axis_index("seq"), lax.axis_index("head")
    tok, width = inner.shape
    sides, _, piece = down.shape
    per_head = n_seq // n_head
    chunk = GROUP * tok
    chunks = n_seq // GROUP
    small = chunks <= 2
    out_head, out_slot = seq // per_head, lax.rem(seq, per_head)
    swap = sides == 2
    partner = lax.rem(seq + n_seq // 2, n_seq)
    sibling = seq + 1 - 2 * lax.rem(seq, 2)

    def loop(count, step, carry=None):
        if small:
            for position in range(count):
                carry = step(position, carry)
            return carry
        return lax.fori_loop(0, count, step, carry)

    loads = [
        pltpu.make_async_copy(source, target, load_sem.at[index])
        for index, (source, target) in enumerate(
            [
                (inner_hbm, inner),
                (erase_hbm, erase),
                (down_hbm.at[:, pl.ds((sides - 1) * piece, piece)], given if swap else down.at[0]),
                (proj_hbm.at[0], proj),
                (conv_hbm, conv),
                (gate_hbm.at[0], gate),
                (gain_hbm, gain),
                (resid_hbm, resid),
            ]
            + ([(down_hbm.at[:, pl.ds(0, piece)], down.at[0])] if swap else [])
        )
    ]
    for load in loads:
        load.start()

    barrier = pltpu.get_barrier_semaphore()
    group = n_seq * n_head
    flat = seq * n_head + head

    def greet(step, carry):
        other = lax.rem(flat + step + 1, group)
        pl.semaphore_signal(
            barrier,
            inc=1,
            device_id={"seq": other // n_head, "head": lax.rem(other, n_head)},
            device_id_type=MESH,
        )
        return carry

    loop(group - 1, greet, 0)

    rows[pl.ds(0, PAD), :] = jnp.zeros((PAD, width), BF16)
    line = lax.broadcasted_iota(jnp.int32, (tok, tok), 0)
    lane = lax.broadcasted_iota(jnp.int32, (tok, tok), 1)
    loads[0].wait()
    loads[1].wait()
    kept = as_column((1 - erase[...]).astype(F32), line == lane)
    own = pl.ds(pl.multiple_of(PAD + seq * tok, PAD), tok)
    rows[own, :] = (inner[...].astype(F32) * kept).astype(BF16)
    for load in loads[2:]:
        load.wait()

    pl.semaphore_wait(barrier, group - 1)

    def row_copy(block, target, slot):
        place = pl.ds(pl.multiple_of(PAD + block * tok, PAD), tok)
        return pltpu.make_async_remote_copy(
            src_ref=rows.at[place],
            dst_ref=rows.at[place],
            send_sem=row_send.at[slot],
            recv_sem=row_recv.at[block],
            device_id={"seq": target},
            device_id_type=MESH,
        )

    def send_rows(step, carry):
        row_copy(seq, lax.rem(seq + 2 * step + 2, n_seq), step).start()
        return carry

    loop(n_seq // 2 - 1, send_rows, 0)
    row_copy(seq, sibling, n_seq // 2 - 1).start()
    give = pltpu.make_async_remote_copy(
        src_ref=given if swap else down.at[0],
        dst_ref=down.at[sides - 1],
        send_sem=down_sem.at[0],
        recv_sem=down_sem.at[1],
        device_id={"seq": partner},
        device_id_type=MESH,
    )
    if swap:
        give.start()

    def forward(step, carry):
        block = lax.rem(seq + n_seq - 2 * step - 2, n_seq)
        row_copy(block, sibling, 0).wait_recv()
        row_copy(block, sibling, n_seq // 2 + step).start()
        return carry

    loop(n_seq // 2 - 1, forward, 0)

    line = lax.broadcasted_iota(jnp.int32, (chunk, chunk), 0)
    lane = lax.broadcasted_iota(jnp.int32, (chunk, chunk), 1)

    def part_copy(side, block, target):
        return pltpu.make_async_remote_copy(
            src_ref=part.at[side, block],
            dst_ref=landed.at[head, side, out_slot],
            send_sem=part_send.at[side, block],
            recv_sem=part_recv.at[head, side, out_slot],
            device_id={"seq": block, "head": target},
            device_id_type=MESH,
        )

    if swap:
        first = 1 - lax.rem(out_head + head, 2)
        routes = [(first, 1 - head), (1 - first, head)]
    else:
        routes = [(0, out_head)]

    def work(index, carry):
        start = index * chunk if small else pl.multiple_of(index * chunk, chunk)
        here = pl.ds(start, chunk)
        for position in range(GROUP):
            block = index * GROUP + position

            @pl.when(lax.rem(seq + block, 2) == 1)
            def _():
                row_copy(block, sibling, 0).wait_recv()

        window = rows[pl.ds(start, chunk + PAD), :].astype(F32)
        convolved = conv[pl.ds(0, 1), :] * window[PAD:]
        for offset in range(1, CONV):
            convolved += conv[pl.ds(offset, 1), :] * pltpu.roll(window, offset, 0)[PAD:]
        half = 0.5 * convolved
        activated = (half + half * jnp.tanh(half)).astype(BF16)
        erased = rows[pl.ds(start + PAD, chunk), :]
        gates = dot_nt(gate[...], activated)
        input_log = 15.0 * jnp.tanh((gates[0:1] + bias_ref[0, 0]) / 15.0)
        forget = gates[1:2] + bias_ref[0, 1]
        forget_log = jnp.minimum(forget, 0.0) - jnp.log1p(jnp.exp(-jnp.abs(forget)))
        summed = jnp.dot(
            jnp.broadcast_to(forget_log, (8, chunk)),
            (line <= lane).astype(F32),
            preferred_element_type=F32,
            precision=lax.Precision.HIGHEST,
        )
        cumulated = summed[0:1]
        last = summed[0:1, chunk - 1 : chunk]
        by_row = as_column(cumulated, line == lane)
        queries = dot_nn(activated, proj[:, :width]).astype(BF16)
        key_rows = (dot_nn(activated, proj[:, width : 2 * width]) * width ** (-0.5)).astype(BF16)
        values = dot_nn(erased, proj[:, 2 * width :]).astype(BF16)
        keys[here, :] = key_rows
        vals[here, :] = values
        exponent = by_row + (input_log - cumulated)
        weights = dot_nt(queries, key_rows) * jnp.exp(jnp.where(line >= lane, exponent, -jnp.inf))
        numerator = dot_nn(weights.astype(BF16), values)

        def earlier(other, total):
            there = pl.ds(other * chunk if small else pl.multiple_of(other * chunk, chunk), chunk)
            tail = tails[other]
            scores = dot_nt(queries, keys[there, :])
            weights = (scores * jnp.exp(by_row + tail[0:1])).astype(BF16)
            tails[other] = tail + last
            return total + dot_nn(weights, vals[there, :])

        numerator = loop(index, earlier, numerator)
        tails[index] = jnp.broadcast_to(last - cumulated + input_log, (8, chunk))
        mean = jnp.mean(numerator, axis=1, keepdims=True)
        centred = numerator - mean
        variance = jnp.mean(centred * centred, axis=1, keepdims=True)
        normed = (centred * lax.rsqrt(variance + 1e-05) * gain[...]).astype(BF16)
        if swap:

            @pl.when(index == 0)
            def _():
                give.wait_recv()

        for side, target in routes:
            product = dot_nn(normed, down[side]).astype(BF16)
            for position in range(GROUP):
                block = index * GROUP + position
                part[side, block] = product[position * tok : (position + 1) * tok]
                mine = (block == seq) & (target == head)

                @pl.when(jnp.logical_not(mine))
                def _():
                    part_copy(side, block, target).start()

                @pl.when(mine)
                def _():
                    pltpu.make_async_copy(
                        part.at[side, block], landed.at[head, side, out_slot], self_sem
                    ).start()

        return carry

    loop(chunks, work, 0)

    for slot in range(per_head):
        for side in range(sides):
            source = lax.rem(head + side, n_head) * per_head + slot
            for other in range(n_head):
                mine = (source == seq) & (other == head)

                @pl.when(jnp.logical_not(mine))
                def _():
                    pltpu.make_async_remote_copy(
                        src_ref=part.at[0, 0],
                        dst_ref=landed.at[other, side, slot],
                        send_sem=part_send.at[0, 0],
                        recv_sem=part_recv.at[other, side, slot],
                        device_id={"seq": sibling},
                        device_id_type=MESH,
                    ).wait_recv()

                @pl.when(mine)
                def _():
                    pltpu.make_async_copy(part.at[0, 0], landed.at[0, 0, 0], self_sem).wait()

            total = landed[0, side, slot].astype(F32)
            for other in range(1, n_head):
                total += landed[other, side, slot].astype(F32)
            place = pl.ds((slot * sides + side) * piece, piece)
            out_ref[0, :, place] = (resid[:, place].astype(F32) + total).astype(BF16)

    def sent_rows(step, carry):
        row_copy(seq, sibling, step).wait_send()
        return carry

    loop(n_seq - 1, sent_rows, 0)
    if swap:
        give.wait_send()

    def sent_parts(block, carry):
        for side, target in routes:

            @pl.when(jnp.logical_not((block == seq) & (target == head)))
            def _():
                part_copy(side, block, target).wait_send()

        return carry

    loop(n_seq, sent_parts, 0)


def body(
    n_seq,
    n_head,
    inner,
    residual_in,
    erase,
    conv_weight,
    qkv_weight,
    gate_weight,
    gate_bias,
    norm_gain,
    down_weight,
):
    tok, width = inner.shape
    columns = down_weight.shape[1]
    tokens = tok * n_seq
    chunk = GROUP * tok
    sides = 2 if n_head == 2 and columns % 256 == 0 else 1
    piece = columns // sides
    per_head = n_seq // n_head
    vmem = pl.BlockSpec(memory_space=pltpu.VMEM)
    anywhere = pl.BlockSpec(memory_space=pl.ANY)
    return pl.pallas_call(
        functools.partial(kernel, n_seq, n_head),
        out_shape=pltpu.VMEM((1, tok, residual_in.shape[1]), BF16),
        in_specs=[anywhere] * 4 + [pl.BlockSpec(memory_space=pltpu.SMEM)] + [anywhere] * 4,
        out_specs=vmem,
        scratch_shapes=[
            pltpu.VMEM(inner.shape, BF16),
            pltpu.VMEM(erase.shape, jnp.int32),
            pltpu.VMEM(conv_weight.shape, F32),
            pltpu.VMEM(gate_weight.shape[1:], BF16),
            pltpu.VMEM((1, width), F32),
            pltpu.VMEM(qkv_weight.shape[1:], BF16),
            pltpu.VMEM((sides, width, piece), BF16),
            pltpu.VMEM((width, piece), BF16),
            pltpu.VMEM(residual_in.shape, BF16),
            pltpu.VMEM((PAD + tokens, width), BF16),
            pltpu.VMEM((tokens, width), BF16),
            pltpu.VMEM((tokens, width), BF16),
            pltpu.VMEM((tokens // chunk, 8, chunk), F32),
            pltpu.VMEM((sides, n_seq, tok, piece), BF16),
            pltpu.VMEM((n_head, sides, per_head, tok, piece), BF16),
            pltpu.SemaphoreType.DMA((9,)),
            pltpu.SemaphoreType.DMA((n_seq,)),
            pltpu.SemaphoreType.DMA((n_seq,)),
            pltpu.SemaphoreType.DMA((2,)),
            pltpu.SemaphoreType.DMA((sides, n_seq)),
            pltpu.SemaphoreType.DMA((n_head, sides, per_head)),
            pltpu.SemaphoreType.DMA,
        ],
        compiler_params=pltpu.CompilerParams(
            collective_id=0, has_side_effects=True, vmem_limit_bytes=62 * 2**20
        ),
    )(
        inner,
        erase,
        conv_weight,
        gate_weight,
        gate_bias,
        norm_gain.reshape(1, width),
        qkv_weight,
        down_weight,
        residual_in,
    )


def solution(mesh):
    in_specs = (
        P("seq", "head"),
        P("seq", "head"),
        P("var", "seq"),
        P(None, "head"),
        P("head", None, None),
        P("head", None, None),
        P("head", None),
        P("head"),
        P("head", "seq"),
    )
    out_specs = P("var", "seq", "head")
    run = functools.partial(body, mesh.shape["seq"], mesh.shape["head"])
    return jax.shard_map(run, mesh=mesh, in_specs=in_specs, out_specs=out_specs, check_vma=False)
```

```python
import functools

import jax
import jax.numpy as jnp
from jax import lax
from jax.experimental import pallas as pl
from jax.experimental.pallas import tpu as pltpu
from jax.sharding import PartitionSpec as P

CONV = 4
PAD = 16
GROUP = 4
MESH = pl.DeviceIdType.MESH
BF16 = jnp.bfloat16
F32 = jnp.float32


def dot_nt(a, b):
    return lax.dot_general(a, b, (((1,), (1,)), ((), ())), preferred_element_type=F32)


def dot_nn(a, b):
    return jnp.dot(a, b, preferred_element_type=F32)


def as_column(row, eye):
    return jnp.sum(jnp.where(eye, row, 0.0), axis=1, keepdims=True)


def kernel(
    n_seq,
    n_head,
    inner_hbm,
    erase_hbm,
    conv_hbm,
    gate_hbm,
    bias_ref,
    gain_hbm,
    proj_hbm,
    down_hbm,
    resid_hbm,
    out_ref,
    inner,
    erase,
    conv,
    gate,
    gain,
    proj,
    down,
    given,
    resid,
    rows,
    keys,
    vals,
    tails,
    part,
    landed,
    load_sem,
    row_send,
    row_recv,
    down_sem,
    part_send,
    part_recv,
    self_sem,
    ready,
):
    seq, head = lax.axis_index("seq"), lax.axis_index("head")
    tok, width = inner.shape
    sides, _, piece = down.shape
    per_head = n_seq // n_head
    chunk = GROUP * tok
    chunks = n_seq // GROUP
    small = chunks <= 2
    out_head, out_slot = seq // per_head, lax.rem(seq, per_head)
    swap = sides == 2
    partner = lax.rem(seq + n_seq // 2, n_seq)
    sibling = seq + 1 - 2 * lax.rem(seq, 2)

    def loop(count, step, carry=None):
        if small:
            for position in range(count):
                carry = step(position, carry)
            return carry
        return lax.fori_loop(0, count, step, carry)

    loads = [
        pltpu.make_async_copy(source, target, load_sem.at[index])
        for index, (source, target) in enumerate(
            [
                (inner_hbm, inner),
                (erase_hbm, erase),
                (down_hbm.at[:, pl.ds((sides - 1) * piece, piece)], given if swap else down.at[0]),
                (proj_hbm.at[0], proj),
                (conv_hbm, conv),
                (gate_hbm.at[0], gate),
                (gain_hbm, gain),
                (resid_hbm, resid),
            ]
            + ([(down_hbm.at[:, pl.ds(0, piece)], down.at[0])] if swap else [])
        )
    ]
    for load in loads:
        load.start()

    barrier = pltpu.get_barrier_semaphore()
    group = n_seq * n_head
    flat = seq * n_head + head

    def greet(step, carry):
        other = lax.rem(flat + step + 1, group)
        pl.semaphore_signal(
            barrier,
            inc=1,
            device_id={"seq": other // n_head, "head": lax.rem(other, n_head)},
            device_id_type=MESH,
        )
        return carry

    if swap:
        near = [{"seq": lax.rem(seq + 2 * k, n_seq)} for k in range(1, n_seq // 2)]
        near += [{"seq": sibling}]
        across = [{"seq": other, "head": 1 - head} for other in (seq, sibling)]
        for target in near + across:
            pl.semaphore_signal(barrier, inc=1, device_id=target, device_id_type=MESH)
    else:
        loop(group - 1, greet, 0)

    rows[pl.ds(0, PAD), :] = jnp.zeros((PAD, width), BF16)
    line = lax.broadcasted_iota(jnp.int32, (tok, tok), 0)
    lane = lax.broadcasted_iota(jnp.int32, (tok, tok), 1)
    loads[0].wait()
    loads[1].wait()
    kept = as_column((1 - erase[...]).astype(F32), line == lane)
    own = pl.ds(pl.multiple_of(PAD + seq * tok, PAD), tok)
    rows[own, :] = (inner[...].astype(F32) * kept).astype(BF16)
    for load in loads[2:]:
        load.wait()

    pl.semaphore_wait(barrier, n_seq // 2 + 2 if swap else group - 1)

    def row_copy(block, target, slot):
        place = pl.ds(pl.multiple_of(PAD + block * tok, PAD), tok)
        return pltpu.make_async_remote_copy(
            src_ref=rows.at[place],
            dst_ref=rows.at[place],
            send_sem=row_send.at[slot],
            recv_sem=row_recv.at[block],
            device_id={"seq": target},
            device_id_type=MESH,
        )

    def send_rows(step, carry):
        row_copy(seq, lax.rem(seq + 2 * step + 2, n_seq), step).start()
        return carry

    loop(n_seq // 2 - 1, send_rows, 0)
    row_copy(seq, sibling, n_seq // 2 - 1).start()
    give = pltpu.make_async_remote_copy(
        src_ref=given if swap else down.at[0],
        dst_ref=down.at[sides - 1],
        send_sem=down_sem.at[0],
        recv_sem=down_sem.at[1],
        device_id={"seq": partner},
        device_id_type=MESH,
    )
    if swap:
        give.start()

    def forward(step, carry):
        block = lax.rem(seq + n_seq - 2 * step - 2, n_seq)
        row_copy(block, sibling, 0).wait_recv()
        row_copy(block, sibling, n_seq // 2 + step).start()
        return carry

    loop(n_seq // 2 - 1, forward, 0)
    if swap:
        for target in across:
            pl.semaphore_signal(ready, inc=1, device_id=target, device_id_type=MESH)

    line = lax.broadcasted_iota(jnp.int32, (chunk, chunk), 0)
    lane = lax.broadcasted_iota(jnp.int32, (chunk, chunk), 1)

    def part_copy(side, block, target):
        return pltpu.make_async_remote_copy(
            src_ref=part.at[side, block],
            dst_ref=landed.at[head, side, out_slot],
            send_sem=part_send.at[side, block],
            recv_sem=part_recv.at[head, side, out_slot],
            device_id={"seq": block, "head": target},
            device_id_type=MESH,
        )

    if swap:
        first = 1 - lax.rem(out_head + head, 2)
        routes = [(first, 1 - head), (1 - first, head)]
    else:
        routes = [(0, out_head)]

    def work(index, carry):
        start = index * chunk if small else pl.multiple_of(index * chunk, chunk)
        here = pl.ds(start, chunk)
        for position in range(GROUP):
            block = index * GROUP + position

            @pl.when(lax.rem(seq + block, 2) == 1)
            def _():
                row_copy(block, sibling, 0).wait_recv()

        window = rows[pl.ds(start, chunk + PAD), :].astype(F32)
        convolved = conv[pl.ds(0, 1), :] * window[PAD:]
        for offset in range(1, CONV):
            convolved += conv[pl.ds(offset, 1), :] * pltpu.roll(window, offset, 0)[PAD:]
        half = 0.5 * convolved
        activated = (half + half * jnp.tanh(half)).astype(BF16)
        erased = rows[pl.ds(start + PAD, chunk), :]
        gates = dot_nt(gate[...], activated)
        input_log = 15.0 * jnp.tanh((gates[0:1] + bias_ref[0, 0]) / 15.0)
        forget = gates[1:2] + bias_ref[0, 1]
        forget_log = jnp.minimum(forget, 0.0) - jnp.log1p(jnp.exp(-jnp.abs(forget)))
        summed = jnp.dot(
            jnp.broadcast_to(forget_log, (8, chunk)),
            (line <= lane).astype(F32),
            preferred_element_type=F32,
            precision=lax.Precision.HIGHEST,
        )
        cumulated = summed[0:1]
        last = summed[0:1, chunk - 1 : chunk]
        by_row = as_column(cumulated, line == lane)
        queries = dot_nn(activated, proj[:, :width]).astype(BF16)
        key_rows = (dot_nn(activated, proj[:, width : 2 * width]) * width ** (-0.5)).astype(BF16)
        values = dot_nn(erased, proj[:, 2 * width :]).astype(BF16)
        keys[here, :] = key_rows
        vals[here, :] = values
        exponent = by_row + (input_log - cumulated)
        weights = dot_nt(queries, key_rows) * jnp.exp(jnp.where(line >= lane, exponent, -jnp.inf))
        numerator = dot_nn(weights.astype(BF16), values)

        def earlier(other, total):
            there = pl.ds(other * chunk if small else pl.multiple_of(other * chunk, chunk), chunk)
            tail = tails[other]
            scores = dot_nt(queries, keys[there, :])
            weights = (scores * jnp.exp(by_row + tail[0:1])).astype(BF16)
            tails[other] = tail + last
            return total + dot_nn(weights, vals[there, :])

        numerator = loop(index, earlier, numerator)
        tails[index] = jnp.broadcast_to(last - cumulated + input_log, (8, chunk))
        mean = jnp.mean(numerator, axis=1, keepdims=True)
        centred = numerator - mean
        variance = jnp.mean(centred * centred, axis=1, keepdims=True)
        normed = (centred * lax.rsqrt(variance + 1e-05) * gain[...]).astype(BF16)
        if swap:

            @pl.when(index == 0)
            def _():
                give.wait_recv()
                pl.semaphore_wait(ready, 2)

        for side, target in routes:
            product = dot_nn(normed, down[side]).astype(BF16)
            for position in range(GROUP):
                block = index * GROUP + position
                part[side, block] = product[position * tok : (position + 1) * tok]
                mine = (block == seq) & (target == head)

                @pl.when(jnp.logical_not(mine))
                def _():
                    part_copy(side, block, target).start()

                @pl.when(mine)
                def _():
                    pltpu.make_async_copy(
                        part.at[side, block], landed.at[head, side, out_slot], self_sem
                    ).start()

        return carry

    loop(chunks, work, 0)

    for slot in range(per_head):
        for side in range(sides):
            source = lax.rem(head + side, n_head) * per_head + slot
            for other in range(n_head):
                mine = (source == seq) & (other == head)

                @pl.when(jnp.logical_not(mine))
                def _():
                    pltpu.make_async_remote_copy(
                        src_ref=part.at[0, 0],
                        dst_ref=landed.at[other, side, slot],
                        send_sem=part_send.at[0, 0],
                        recv_sem=part_recv.at[other, side, slot],
                        device_id={"seq": sibling},
                        device_id_type=MESH,
                    ).wait_recv()

                @pl.when(mine)
                def _():
                    pltpu.make_async_copy(part.at[0, 0], landed.at[0, 0, 0], self_sem).wait()

            total = landed[0, side, slot].astype(F32)
            for other in range(1, n_head):
                total += landed[other, side, slot].astype(F32)
            place = pl.ds((slot * sides + side) * piece, piece)
            out_ref[0, :, place] = (resid[:, place].astype(F32) + total).astype(BF16)

    def sent_rows(step, carry):
        row_copy(seq, sibling, step).wait_send()
        return carry

    loop(n_seq - 1, sent_rows, 0)
    if swap:
        give.wait_send()

    def sent_parts(block, carry):
        for side, target in routes:

            @pl.when(jnp.logical_not((block == seq) & (target == head)))
            def _():
                part_copy(side, block, target).wait_send()

        return carry

    loop(n_seq, sent_parts, 0)


def body(
    n_seq,
    n_head,
    inner,
    residual_in,
    erase,
    conv_weight,
    qkv_weight,
    gate_weight,
    gate_bias,
    norm_gain,
    down_weight,
):
    tok, width = inner.shape
    columns = down_weight.shape[1]
    tokens = tok * n_seq
    chunk = GROUP * tok
    sides = 2 if n_head == 2 and columns % 256 == 0 else 1
    piece = columns // sides
    per_head = n_seq // n_head
    vmem = pl.BlockSpec(memory_space=pltpu.VMEM)
    anywhere = pl.BlockSpec(memory_space=pl.ANY)
    return pl.pallas_call(
        functools.partial(kernel, n_seq, n_head),
        out_shape=pltpu.VMEM((1, tok, residual_in.shape[1]), BF16),
        in_specs=[anywhere] * 4 + [pl.BlockSpec(memory_space=pltpu.SMEM)] + [anywhere] * 4,
        out_specs=vmem,
        scratch_shapes=[
            pltpu.VMEM(inner.shape, BF16),
            pltpu.VMEM(erase.shape, jnp.int32),
            pltpu.VMEM(conv_weight.shape, F32),
            pltpu.VMEM(gate_weight.shape[1:], BF16),
            pltpu.VMEM((1, width), F32),
            pltpu.VMEM(qkv_weight.shape[1:], BF16),
            pltpu.VMEM((sides, width, piece), BF16),
            pltpu.VMEM((width, piece), BF16),
            pltpu.VMEM(residual_in.shape, BF16),
            pltpu.VMEM((PAD + tokens, width), BF16),
            pltpu.VMEM((tokens, width), BF16),
            pltpu.VMEM((tokens, width), BF16),
            pltpu.VMEM((tokens // chunk, 8, chunk), F32),
            pltpu.VMEM((sides, n_seq, tok, piece), BF16),
            pltpu.VMEM((n_head, sides, per_head, tok, piece), BF16),
            pltpu.SemaphoreType.DMA((9,)),
            pltpu.SemaphoreType.DMA((n_seq,)),
            pltpu.SemaphoreType.DMA((n_seq,)),
            pltpu.SemaphoreType.DMA((2,)),
            pltpu.SemaphoreType.DMA((sides, n_seq)),
            pltpu.SemaphoreType.DMA((n_head, sides, per_head)),
            pltpu.SemaphoreType.DMA,
            pltpu.SemaphoreType.REGULAR,
        ],
        compiler_params=pltpu.CompilerParams(
            collective_id=0, has_side_effects=True, vmem_limit_bytes=62 * 2**20
        ),
    )(
        inner,
        erase,
        conv_weight,
        gate_weight,
        gate_bias,
        norm_gain.reshape(1, width),
        qkv_weight,
        down_weight,
        residual_in,
    )


def solution(mesh):
    in_specs = (
        P("seq", "head"),
        P("seq", "head"),
        P("var", "seq"),
        P(None, "head"),
        P("head", None, None),
        P("head", None, None),
        P("head", None),
        P("head"),
        P("head", "seq"),
    )
    out_specs = P("var", "seq", "head")
    run = functools.partial(body, mesh.shape["seq"], mesh.shape["head"])
    return jax.shard_map(run, mesh=mesh, in_specs=in_specs, out_specs=out_specs, check_vma=False)
```

```python
import functools

import jax
import jax.numpy as jnp
from jax import lax
from jax.experimental import pallas as pl
from jax.experimental.pallas import tpu as pltpu
from jax.sharding import PartitionSpec as P

CONV = 4
PAD = 16
GROUP = 4
MESH = pl.DeviceIdType.MESH
BF16 = jnp.bfloat16
F32 = jnp.float32


def dot_nt(a, b):
    return lax.dot_general(a, b, (((1,), (1,)), ((), ())), preferred_element_type=F32)


def dot_nn(a, b):
    return jnp.dot(a, b, preferred_element_type=F32)


def as_column(row, eye):
    return jnp.sum(jnp.where(eye, row, 0.0), axis=1, keepdims=True)


def kernel(
    n_seq,
    n_head,
    inner_hbm,
    erase_hbm,
    conv_hbm,
    gate_hbm,
    bias_ref,
    gain_hbm,
    proj_hbm,
    down_hbm,
    resid_hbm,
    out_ref,
    inner,
    erase,
    conv,
    gate,
    gain,
    proj,
    down,
    given,
    resid,
    rows,
    keys,
    vals,
    tails,
    part,
    landed,
    load_sem,
    row_send,
    row_recv,
    down_sem,
    part_send,
    part_recv,
    self_sem,
    ready,
):
    seq, head = lax.axis_index("seq"), lax.axis_index("head")
    tok, width = inner.shape
    sides, _, piece = down.shape
    per_head = n_seq // n_head
    chunk = GROUP * tok
    chunks = n_seq // GROUP
    small = chunks <= 2
    out_head, out_slot = seq // per_head, lax.rem(seq, per_head)
    swap = sides == 2
    partner = lax.rem(seq + n_seq // 2, n_seq)
    sibling = seq + 1 - 2 * lax.rem(seq, 2)

    def loop(count, step, carry=None):
        if small:
            for position in range(count):
                carry = step(position, carry)
            return carry
        return lax.fori_loop(0, count, step, carry)

    barrier = pltpu.get_barrier_semaphore()
    group = n_seq * n_head
    flat = seq * n_head + head

    def greet(step, carry):
        other = lax.rem(flat + step + 1, group)
        pl.semaphore_signal(
            barrier,
            inc=1,
            device_id={"seq": other // n_head, "head": lax.rem(other, n_head)},
            device_id_type=MESH,
        )
        return carry

    if swap:
        near = [{"seq": lax.rem(seq + 2 * k, n_seq)} for k in range(1, n_seq // 2)]
        near += [{"seq": sibling}]
        across = [{"seq": other, "head": 1 - head} for other in (seq, sibling)]
        for target in near + across:
            pl.semaphore_signal(barrier, inc=1, device_id=target, device_id_type=MESH)
    else:
        loop(group - 1, greet, 0)

    loads = [
        pltpu.make_async_copy(source, target, load_sem.at[index])
        for index, (source, target) in enumerate(
            [
                (inner_hbm, inner),
                (erase_hbm, erase),
                (down_hbm.at[:, pl.ds((sides - 1) * piece, piece)], given if swap else down.at[0]),
                (proj_hbm.at[0], proj),
                (conv_hbm, conv),
                (gate_hbm.at[0], gate),
                (gain_hbm, gain),
                (resid_hbm, resid),
            ]
            + ([(down_hbm.at[:, pl.ds(0, piece)], down.at[0])] if swap else [])
        )
    ]
    for load in loads:
        load.start()

    rows[pl.ds(0, PAD), :] = jnp.zeros((PAD, width), BF16)
    line = lax.broadcasted_iota(jnp.int32, (tok, tok), 0)
    lane = lax.broadcasted_iota(jnp.int32, (tok, tok), 1)
    loads[0].wait()
    loads[1].wait()
    kept = as_column((1 - erase[...]).astype(F32), line == lane)
    own = pl.ds(pl.multiple_of(PAD + seq * tok, PAD), tok)
    rows[own, :] = (inner[...].astype(F32) * kept).astype(BF16)
    pl.semaphore_wait(barrier, n_seq // 2 + 2 if swap else group - 1)

    def row_copy(block, target, slot):
        place = pl.ds(pl.multiple_of(PAD + block * tok, PAD), tok)
        return pltpu.make_async_remote_copy(
            src_ref=rows.at[place],
            dst_ref=rows.at[place],
            send_sem=row_send.at[slot],
            recv_sem=row_recv.at[block],
            device_id={"seq": target},
            device_id_type=MESH,
        )

    def send_rows(step, carry):
        row_copy(seq, lax.rem(seq + 2 * step + 2, n_seq), step).start()
        return carry

    loop(n_seq // 2 - 1, send_rows, 0)
    row_copy(seq, sibling, n_seq // 2 - 1).start()
    give = pltpu.make_async_remote_copy(
        src_ref=given if swap else down.at[0],
        dst_ref=down.at[sides - 1],
        send_sem=down_sem.at[0],
        recv_sem=down_sem.at[1],
        device_id={"seq": partner},
        device_id_type=MESH,
    )
    loads[2].wait()
    if swap:
        give.start()

    def forward(step, carry):
        block = lax.rem(seq + n_seq - 2 * step - 2, n_seq)
        row_copy(block, sibling, 0).wait_recv()
        row_copy(block, sibling, n_seq // 2 + step).start()
        return carry

    loop(n_seq // 2 - 1, forward, 0)
    if swap:
        for target in across:
            pl.semaphore_signal(ready, inc=1, device_id=target, device_id_type=MESH)

    for load in loads[3:]:
        load.wait()
    line = lax.broadcasted_iota(jnp.int32, (chunk, chunk), 0)
    lane = lax.broadcasted_iota(jnp.int32, (chunk, chunk), 1)

    def part_copy(side, block, target):
        return pltpu.make_async_remote_copy(
            src_ref=part.at[side, block],
            dst_ref=landed.at[head, side, out_slot],
            send_sem=part_send.at[side, block],
            recv_sem=part_recv.at[head, side, out_slot],
            device_id={"seq": block, "head": target},
            device_id_type=MESH,
        )

    if swap:
        first = 1 - lax.rem(out_head + head, 2)
        routes = [(first, 1 - head), (1 - first, head)]
    else:
        routes = [(0, out_head)]

    def work(index, carry):
        start = index * chunk if small else pl.multiple_of(index * chunk, chunk)
        here = pl.ds(start, chunk)
        for position in range(GROUP):
            block = index * GROUP + position

            @pl.when(lax.rem(seq + block, 2) == 1)
            def _():
                row_copy(block, sibling, 0).wait_recv()

        window = rows[pl.ds(start, chunk + PAD), :].astype(F32)
        convolved = conv[pl.ds(0, 1), :] * window[PAD:]
        for offset in range(1, CONV):
            convolved += conv[pl.ds(offset, 1), :] * pltpu.roll(window, offset, 0)[PAD:]
        half = 0.5 * convolved
        activated = (half + half * jnp.tanh(half)).astype(BF16)
        erased = rows[pl.ds(start + PAD, chunk), :]
        gates = dot_nt(gate[...], activated)
        input_log = 15.0 * jnp.tanh((gates[0:1] + bias_ref[0, 0]) / 15.0)
        forget = gates[1:2] + bias_ref[0, 1]
        forget_log = jnp.minimum(forget, 0.0) - jnp.log1p(jnp.exp(-jnp.abs(forget)))
        summed = jnp.dot(
            jnp.broadcast_to(forget_log, (8, chunk)),
            (line <= lane).astype(F32),
            preferred_element_type=F32,
            precision=lax.Precision.HIGHEST,
        )
        cumulated = summed[0:1]
        last = summed[0:1, chunk - 1 : chunk]
        by_row = as_column(cumulated, line == lane)
        queries = dot_nn(activated, proj[:, :width]).astype(BF16)
        key_rows = (dot_nn(activated, proj[:, width : 2 * width]) * width ** (-0.5)).astype(BF16)
        values = dot_nn(erased, proj[:, 2 * width :]).astype(BF16)
        keys[here, :] = key_rows
        vals[here, :] = values
        exponent = by_row + (input_log - cumulated)
        weights = dot_nt(queries, key_rows) * jnp.exp(jnp.where(line >= lane, exponent, -jnp.inf))
        numerator = dot_nn(weights.astype(BF16), values)

        def earlier(other, total):
            there = pl.ds(other * chunk if small else pl.multiple_of(other * chunk, chunk), chunk)
            tail = tails[other]
            scores = dot_nt(queries, keys[there, :])
            weights = (scores * jnp.exp(by_row + tail[0:1])).astype(BF16)
            tails[other] = tail + last
            return total + dot_nn(weights, vals[there, :])

        numerator = loop(index, earlier, numerator)
        tails[index] = jnp.broadcast_to(last - cumulated + input_log, (8, chunk))
        mean = jnp.mean(numerator, axis=1, keepdims=True)
        centred = numerator - mean
        variance = jnp.mean(centred * centred, axis=1, keepdims=True)
        normed = (centred * lax.rsqrt(variance + 1e-05) * gain[...]).astype(BF16)
        if swap:

            @pl.when(index == 0)
            def _():
                give.wait_recv()
                pl.semaphore_wait(ready, 2)

        for side, target in routes:
            product = dot_nn(normed, down[side]).astype(BF16)
            for position in range(GROUP):
                block = index * GROUP + position
                part[side, block] = product[position * tok : (position + 1) * tok]
                mine = (block == seq) & (target == head)

                @pl.when(jnp.logical_not(mine))
                def _():
                    part_copy(side, block, target).start()

                @pl.when(mine)
                def _():
                    pltpu.make_async_copy(
                        part.at[side, block], landed.at[head, side, out_slot], self_sem
                    ).start()

        return carry

    loop(chunks, work, 0)

    for slot in range(per_head):
        for side in range(sides):
            source = lax.rem(head + side, n_head) * per_head + slot
            for other in range(n_head):
                mine = (source == seq) & (other == head)

                @pl.when(jnp.logical_not(mine))
                def _():
                    pltpu.make_async_remote_copy(
                        src_ref=part.at[0, 0],
                        dst_ref=landed.at[other, side, slot],
                        send_sem=part_send.at[0, 0],
                        recv_sem=part_recv.at[other, side, slot],
                        device_id={"seq": sibling},
                        device_id_type=MESH,
                    ).wait_recv()

                @pl.when(mine)
                def _():
                    pltpu.make_async_copy(part.at[0, 0], landed.at[0, 0, 0], self_sem).wait()

            total = landed[0, side, slot].astype(F32)
            for other in range(1, n_head):
                total += landed[other, side, slot].astype(F32)
            place = pl.ds((slot * sides + side) * piece, piece)
            out_ref[0, :, place] = (resid[:, place].astype(F32) + total).astype(BF16)

    def sent_rows(step, carry):
        row_copy(seq, sibling, step).wait_send()
        return carry

    loop(n_seq - 1, sent_rows, 0)
    if swap:
        give.wait_send()

    def sent_parts(block, carry):
        for side, target in routes:

            @pl.when(jnp.logical_not((block == seq) & (target == head)))
            def _():
                part_copy(side, block, target).wait_send()

        return carry

    loop(n_seq, sent_parts, 0)


def body(
    n_seq,
    n_head,
    inner,
    residual_in,
    erase,
    conv_weight,
    qkv_weight,
    gate_weight,
    gate_bias,
    norm_gain,
    down_weight,
):
    tok, width = inner.shape
    columns = down_weight.shape[1]
    tokens = tok * n_seq
    chunk = GROUP * tok
    sides = 2 if n_head == 2 and columns % 256 == 0 else 1
    piece = columns // sides
    per_head = n_seq // n_head
    vmem = pl.BlockSpec(memory_space=pltpu.VMEM)
    anywhere = pl.BlockSpec(memory_space=pl.ANY)
    return pl.pallas_call(
        functools.partial(kernel, n_seq, n_head),
        out_shape=pltpu.VMEM((1, tok, residual_in.shape[1]), BF16),
        in_specs=[anywhere] * 4 + [pl.BlockSpec(memory_space=pltpu.SMEM)] + [anywhere] * 4,
        out_specs=vmem,
        scratch_shapes=[
            pltpu.VMEM(inner.shape, BF16),
            pltpu.VMEM(erase.shape, jnp.int32),
            pltpu.VMEM(conv_weight.shape, F32),
            pltpu.VMEM(gate_weight.shape[1:], BF16),
            pltpu.VMEM((1, width), F32),
            pltpu.VMEM(qkv_weight.shape[1:], BF16),
            pltpu.VMEM((sides, width, piece), BF16),
            pltpu.VMEM((width, piece), BF16),
            pltpu.VMEM(residual_in.shape, BF16),
            pltpu.VMEM((PAD + tokens, width), BF16),
            pltpu.VMEM((tokens, width), BF16),
            pltpu.VMEM((tokens, width), BF16),
            pltpu.VMEM((tokens // chunk, 8, chunk), F32),
            pltpu.VMEM((sides, n_seq, tok, piece), BF16),
            pltpu.VMEM((n_head, sides, per_head, tok, piece), BF16),
            pltpu.SemaphoreType.DMA((9,)),
            pltpu.SemaphoreType.DMA((n_seq,)),
            pltpu.SemaphoreType.DMA((n_seq,)),
            pltpu.SemaphoreType.DMA((2,)),
            pltpu.SemaphoreType.DMA((sides, n_seq)),
            pltpu.SemaphoreType.DMA((n_head, sides, per_head)),
            pltpu.SemaphoreType.DMA,
            pltpu.SemaphoreType.REGULAR,
        ],
        compiler_params=pltpu.CompilerParams(
            collective_id=0, has_side_effects=True, vmem_limit_bytes=62 * 2**20
        ),
    )(
        inner,
        erase,
        conv_weight,
        gate_weight,
        gate_bias,
        norm_gain.reshape(1, width),
        qkv_weight,
        down_weight,
        residual_in,
    )


def solution(mesh):
    in_specs = (
        P("seq", "head"),
        P("seq", "head"),
        P("var", "seq"),
        P(None, "head"),
        P("head", None, None),
        P("head", None, None),
        P("head", None),
        P("head"),
        P("head", "seq"),
    )
    out_specs = P("var", "seq", "head")
    run = functools.partial(body, mesh.shape["seq"], mesh.shape["head"])
    return jax.shard_map(run, mesh=mesh, in_specs=in_specs, out_specs=out_specs, check_vma=False)
```
